256 devices in a mesh: section: 8 (over z), row: 2 (over core), col: 16 (over y, x).
Axes of the slice: x: 4, y: 4, z: 8, core: 2. Of those that a mesh axis runs over, the one named last changes fastest.
Arguments:
- in_flight: bfloat16 [8, 1024, 6144], P('section', 'row', 'col'), may hold values from -6 to 6
- injected: bfloat16 [1, 1024, 6144], P(None, 'row', 'col'), may hold values from -6 to 6
- weights: bfloat16 [8, 3, 6144, 6144], P('section', None, 'row', 'col'), may hold values from -0.078125 to 0.078125
Outputs:
- segment_out: bfloat16 [8, 1024, 6144], P('section', 'row', 'col')
The draws below stay inside these ranges and needn't reach their ends.
All inputs are finite; a program needn't handle non-finite values.
Results may differ from the reference program's by a relative error of at most 0.0049.
Values may be sent and summed in bfloat16 or wider, within the bound.
No kernel may reach another device: no remote copies, remote signals or barrier semaphores. Data moves between devices by JAX's collectives and lax.ppermute only.
A program may use at most 128 MiB of HBM per device.

```python
import jax
import jax.numpy as jnp
from jax import lax

D = 6144
TOK = 1024
TICKS = 2
SECTIONS = 8


def block_levels(rng, dims, shards, least, high):
    def one(axis_at, shards_of):
        heights = jax.random.uniform(jax.random.fold_in(jax.random.fold_in(rng, 6), axis_at), (shards_of,), jnp.float32, least / len(shards), high / len(shards))
        return jnp.repeat(jnp.exp(heights), dims[axis_at] // shards_of).reshape((-1,) + (1,) * (len(dims) - axis_at - 1))

    loudness = one(*shards[0])
    for cut in shards[1:]:
        loudness = loudness * one(*cut)
    return loudness


def normal_values(stream_key, dims, width, reach, split=(), held_as=jnp.bfloat16):
    array = width * jax.random.normal(stream_key, dims, jnp.float32)
    if split:
        array = array * block_levels(stream_key, dims, split, -0.22, 0.18)
    return jnp.clip(array, -reach, reach).astype(held_as)


def setup_inputs(seed: int = 0) -> dict:
    key_list = jax.random.split(jax.random.key(seed), 4)
    return {
        "in_flight": normal_values(key_list[0], (SECTIONS, TOK, D), 1.0, 6.0, ((0, 8), (1, 2), (2, 16))),
        "injected": normal_values(key_list[1], (TICKS - 1, TOK, D), 1.0, 6.0, ((1, 2), (2, 16))),
        "weights": normal_values(key_list[2], (SECTIONS, 3, D, D), D ** -0.5, 0.078125, ((0, 8), (2, 2), (3, 16))),
    }


def apply_block(pair):
    acts, weight = pair
    first = jnp.dot(acts, weight[0], preferred_element_type=jnp.float32)
    second = jnp.dot(acts, weight[1], preferred_element_type=jnp.float32)
    third = jnp.dot(acts, weight[2], preferred_element_type=jnp.float32)
    branch = jax.nn.sigmoid(third) * jax.nn.gelu(first, approximate=True) * second
    return (acts.astype(jnp.float32) + branch).astype(jnp.bfloat16)


def reference(in_flight, injected, weights):
    state = in_flight
    output = lax.map(apply_block, (state, weights))
    for tick in range(1, TICKS):
        state = jnp.concatenate([injected[tick - 1][None], output[:-1]], axis=0)
        output = lax.map(apply_block, (state, weights))
    return output
```

```python
import functools

import jax
import jax.numpy as jnp
from jax import lax
from jax.experimental import pallas as pl
from jax.experimental.pallas import tpu as pltpu
from jax.sharding import PartitionSpec as P

TICKS = 2
SIDE = 4
PLANE = ("row", "col")


def ring_pairs(step, first):
    pairs = []
    for core in range(2):
        for col in range(SIDE * SIDE):
            y, x = divmod(col, SIDE)
            if (core == 0) == first:
                x = (x + step) % SIDE
            else:
                y = (y + step) % SIDE
            pairs.append((core * SIDE * SIDE + col, core * SIDE * SIDE + y * SIDE + x))
    return pairs


def shift(value, step, first):
    return lax.ppermute(value, PLANE, ring_pairs(step, first))


def block_ids(offsets):
    core, col = lax.axis_index("row"), lax.axis_index("col")
    y, x = col // SIDE, col % SIDE
    ids = []
    for first, second in offsets:
        along_x = jnp.where(core == 0, first, second)
        along_y = jnp.where(core == 0, second, first)
        block = (y + along_y + SIDE) % SIDE * SIDE + (x + along_x + SIDE) % SIDE
        ids += [(block // 8 + core) % 2, block % 8]
    last = lax.axis_index("section") == lax.axis_size("section") - 1
    return jnp.stack(ids + [last.astype(jnp.int32)]).astype(jnp.int32)


def products_kernel(groups, carried, final, injects, *refs):
    refs = list(refs)
    ids = refs.pop(0)
    xs = [refs.pop(0) for _ in groups]
    own, other = refs.pop(0), refs.pop(0)
    acc_in = refs.pop(0) if carried else None
    acts_in = refs.pop(0) if final else None
    inj_in = refs.pop(0) if injects else None
    out = refs.pop(0)
    x_buf, w_buf, acc, x_sem, w_sem, a_sem = refs[:6]
    rest = refs[6:]
    depth = own.shape[1] // 8
    places = [(g, i) for g, n in enumerate(groups) for i in range(n)]
    x_copies = [
        pltpu.make_async_copy(xs[g].at[i], x_buf.at[b], x_sem.at[b]) for b, (g, i) in enumerate(places)
    ]

    def w_copy(source, b):
        rows = pl.ds(pl.multiple_of(ids[2 * b + 1] * depth, depth), depth)
        return pltpu.make_async_copy(source.at[:, rows, :], w_buf.at[b], w_sem.at[b])

    def start(b):
        x_copies[b].start()

        @pl.when(ids[2 * b] == 0)
        def _():
            w_copy(own, b).start()

        @pl.when(ids[2 * b] != 0)
        def _():
            w_copy(other, b).start()

    start(0)
    start(1)
    if carried:
        acc_copy = pltpu.make_async_copy(acc_in, acc, a_sem.at[0])
        acc_copy.start()
    for b in range(2, len(places)):
        start(b)
    if final:
        acts_copy = pltpu.make_async_copy(acts_in, rest[0], a_sem.at[1])
        acts_copy.start()
    if injects:
        inj_copy = pltpu.make_async_copy(inj_in, rest[1], a_sem.at[2])
        inj_copy.start()
    for pair in range(len(places) // 2):
        for b in (2 * pair, 2 * pair + 1):
            x_copies[b].wait()
            w_copy(own, b).wait()
        x = jnp.concatenate([x_buf[2 * pair], x_buf[2 * pair + 1]], axis=1)
        if carried and pair == 0:
            acc_copy.wait()
        for k in range(3):
            w = jnp.concatenate([w_buf[2 * pair, k], w_buf[2 * pair + 1, k]], axis=0)
            part = jnp.dot(x, w, preferred_element_type=jnp.float32)
            if carried or pair > 0:
                part = acc[k] + part
            acc[k] = part
    if not final:
        out_copy = pltpu.make_async_copy(acc, out, a_sem.at[1])
        out_copy.start()
        out_copy.wait()
        return
    acts_copy.wait()
    if injects:
        inj_copy.wait()
    rows = 64

    @pl.loop(0, acc.shape[1] // rows)
    def _(i):
        at = pl.ds(pl.multiple_of(i * rows, rows), rows)
        first, second, third = acc[0, at], acc[1, at], acc[2, at]
        gate = 1.0 / (1.0 + jnp.exp(-third))
        cubic = 0.7978845608 * (first + 0.044715 * (first * first * first))
        value = rest[0][at].astype(jnp.float32) + gate * (0.5 * first * (1.0 + jnp.tanh(cubic))) * second
        value = value.astype(jnp.bfloat16)
        if injects:
            value = jnp.where(ids[2 * len(places)] != 0, rest[1][at], value)
        out[at] = value


def products(ids, groups, own, other, acc=None, acts=None, injected=None):
    tokens, width = groups[0].shape[1:]
    counts = tuple(g.shape[0] for g in groups)
    blocks = sum(counts)
    final = acts is not None
    injects = injected is not None
    operands = [ids, *groups, own, other]
    aliases = {}
    if acc is not None:
        if not final:
            aliases = {len(operands): 0}
        operands.append(acc)
    operands += [v for v in (acts, injected) if v is not None]
    scratch = [
        pltpu.VMEM((blocks, tokens, width), jnp.bfloat16),
        pltpu.VMEM((blocks, 3, width, width), jnp.bfloat16),
        pltpu.VMEM((3, tokens, width), jnp.float32),
        pltpu.SemaphoreType.DMA((blocks,)),
        pltpu.SemaphoreType.DMA((blocks,)),
        pltpu.SemaphoreType.DMA((3,)),
    ]
    scratch += [pltpu.VMEM((tokens, width), jnp.bfloat16)] * (final + injects)
    return pl.pallas_call(
        functools.partial(products_kernel, counts, acc is not None, final, injects),
        out_shape=jax.ShapeDtypeStruct((tokens, width), jnp.bfloat16)
        if final
        else jax.ShapeDtypeStruct((3, tokens, width), jnp.float32),
        in_specs=[pl.BlockSpec(memory_space=pltpu.SMEM)]
        + [pl.BlockSpec(memory_space=pl.ANY)] * (len(operands) - 1),
        out_specs=pl.BlockSpec(memory_space=pltpu.VMEM if final else pl.ANY),
        scratch_shapes=scratch,
        input_output_aliases=aliases,
        compiler_params=pltpu.CompilerParams(vmem_limit_bytes=24 * 1024 * 1024),
        cost_estimate=pl.CostEstimate(
            flops=2 * blocks * tokens * width * width * 3,
            bytes_accessed=2 * blocks * width * (tokens + 3 * width),
            transcendentals=0,
        ),
    )(*operands)


def block(acts, own, other, injected=None):
    near = [acts] + [shift(acts, step, True) for step in (1, 3, 2)]
    low, high = jnp.stack(near[:2]), jnp.stack(near[2:])
    low_at, high_at = (0, -1), (1, 2)

    def ids(*parts):
        return block_ids([(one, two) for at, two in parts for one in at])

    up_low, down_high = shift(low, 1, False), shift(high, 3, False)
    up_high, down_low = shift(high, 1, False), shift(low, 3, False)
    far_low, far_high = shift(up_low, 1, False), shift(down_high, 3, False)
    acc = products(ids((low_at, 0), (high_at, 0)), [low, high], own, other)
    acc = products(ids((low_at, -1), (high_at, 1)), [up_low, down_high], own, other, acc)
    acc = products(ids((high_at, -1), (low_at, 1)), [up_high, down_low], own, other, acc)
    return products(
        ids((low_at, 2), (high_at, 2)), [far_low, far_high], own, other, acc, acts, injected
    )


def body(in_flight, injected, weights):
    own = weights[0]
    other = lax.ppermute(own, "row", [(0, 1), (1, 0)])
    count = lax.axis_size("section")
    acts = in_flight[0]
    for tick in range(TICKS - 1):
        output = block(acts, own, other, injected[tick])
        acts = lax.ppermute(output, "section", [(s, (s + 1) % count) for s in range(count)])
    return block(acts, own, other)[None]


def solution(mesh):
    placed = (P("section", "row", "col"), P(None, "row", "col"), P("section", None, "row", "col"))
    return jax.shard_map(
        body, mesh=mesh, in_specs=placed, out_specs=P("section", "row", "col"), check_vma=False
    )
```

```python
import functools

import jax
import jax.numpy as jnp
from jax import lax
from jax.experimental import pallas as pl
from jax.experimental.pallas import tpu as pltpu
from jax.sharding import PartitionSpec as P

SIDE = 4
PLANE = ("row", "col")
NEAR = (0, -1, 1, 2)
VMEM = pl.BlockSpec(memory_space=pltpu.VMEM)
ANY = pl.BlockSpec(memory_space=pl.ANY)


def ring_pairs(step, first):
    pairs = []
    for core in range(2):
        for col in range(SIDE * SIDE):
            y, x = divmod(col, SIDE)
            if (core == 0) == first:
                x = (x + step) % SIDE
            else:
                y = (y + step) % SIDE
            pairs.append((core * SIDE * SIDE + col, core * SIDE * SIDE + y * SIDE + x))
    return pairs


def shift(value, step, first):
    return lax.ppermute(value, PLANE, ring_pairs(step, first))


def relay(output):
    count = lax.axis_size("section")
    return lax.ppermute(output, "section", [(s, (s + 1) % count) for s in range(count)])


def block_ids():
    core, col = lax.axis_index("row"), lax.axis_index("col")
    y, x = col // SIDE, col % SIDE
    ids = []
    for second in NEAR:
        for first in NEAR:
            along_x = first + core * (second - first)
            along_y = second + core * (first - second)
            block = (y + along_y + SIDE) % SIDE * SIDE + (x + along_x + SIDE) % SIDE
            ids.append(((block // 8 + core) % 2, block % 8))
    return ids


def in_vmem(value):
    return pltpu.with_memory_space_constraint(value, pltpu.VMEM)


def in_hbm(value):
    return pltpu.with_memory_space_constraint(value, pltpu.HBM)


def run(kernel, out_shape, operands, after=(), specs=None, scratch=(), megabytes=4):
    operands = list(operands)
    if specs is None:
        specs = [VMEM] * len(operands)
        operands = [in_vmem(v) for v in operands]
    count = len(operands)

    def body(*refs):
        kernel(*refs[:count], *refs[count + len(after) :])

    return pl.pallas_call(
        body,
        out_shape=out_shape,
        in_specs=specs + [VMEM] * len(after),
        out_specs=jax.tree.map(lambda _: VMEM, out_shape),
        scratch_shapes=list(scratch),
        compiler_params=pltpu.CompilerParams(vmem_limit_bytes=megabytes * 1024 * 1024),
        cost_estimate=pl.CostEstimate(flops=1, bytes_accessed=1, transcendentals=0),
    )(*operands, *map(in_vmem, after))


def arrange(own, other, after):
    _, half, width = own.shape
    depth = half // 8

    def kernel(own, other, out, sems):
        ids = block_ids()

        def copy(source, block, k):
            rows = pl.ds(pl.multiple_of(ids[block][1] * depth, depth), depth)
            place = out.at[pl.ds(block * depth, depth), pl.ds(k * width, width)]
            return pltpu.make_async_copy(source.at[k, rows, :], place, sems.at[block, k])

        for block in range(SIDE * SIDE):

            @pl.when(ids[block][0] == 0)
            def _():
                for k in range(3):
                    copy(own, block, k).start()

            @pl.when(ids[block][0] != 0)
            def _():
                for k in range(3):
                    copy(other, block, k).start()

        for block in range(SIDE * SIDE):
            for k in range(3):
                copy(own, block, k).wait()

    return run(
        kernel,
        pltpu.VMEM((2 * half, 3 * width), jnp.bfloat16),
        [in_hbm(own), in_vmem(other)],
        after,
        specs=[ANY, VMEM],
        scratch=[pltpu.SemaphoreType.DMA((SIDE * SIDE, 3))],
    )


def bring_in(values):
    def kernel(*refs):
        sems = refs[-1]
        count = len(values)
        copies = [
            pltpu.make_async_copy(refs[i], refs[count + i], sems.at[i]) for i in range(count)
        ]
        for copy in copies:
            copy.start()
        for copy in copies:
            copy.wait()

    return run(
        kernel,
        tuple(pltpu.VMEM(v.shape, v.dtype) for v in values),
        [in_hbm(v) for v in values],
        specs=[ANY] * len(values),
        scratch=[pltpu.SemaphoreType.DMA((len(values),))],
    )


def stack(parts, cut, after):
    def kernel(*refs):
        for i, ref in enumerate(refs[:-1]):
            refs[-1][i] = ref[cut]

    tokens, width = cut.stop - cut.start, parts[0].shape[1]
    return run(kernel, pltpu.VMEM((len(parts), tokens, width), jnp.bfloat16), parts, after)


def pick(up, down, after):
    def kernel(up, down, far_up, far_down):
        far_up[...] = up[:2]
        far_down[...] = down[2:]

    one = pltpu.VMEM((2, *up.shape[1:]), jnp.bfloat16)
    return run(kernel, (one, one), [up, down], after)


def same(value, after):
    def kernel(value, out):
        out[...] = value[...]

    return run(kernel, pltpu.VMEM(value.shape, value.dtype), [value], after)


def gathered(refs):
    return jnp.concatenate([ref[i] for ref in refs for i in range(ref.shape[0])], axis=1)


def nearest(near, weights, after):
    def kernel(near, weights, out):
        acts = gathered((near,))
        out[...] = jnp.dot(acts, weights[: acts.shape[1]], preferred_element_type=jnp.float32)

    tokens, width = near.shape[1:]
    kind = pltpu.VMEM((tokens, 3 * width), jnp.float32)
    return run(kernel, kind, [near, weights], after, megabytes=16)


def next_ones(up, down, weights, acc, after):
    def kernel(up, down, weights, acc, out):
        acts = gathered((up, down))
        rows = slice(acts.shape[1] // 2, acts.shape[1] * 3 // 2)
        out[...] = acc[...] + jnp.dot(acts, weights[rows], preferred_element_type=jnp.float32)

    kind = pltpu.VMEM(acc.shape, acc.dtype)
    return run(kernel, kind, [up, down, weights, acc], after, megabytes=16)


def finished(far_up, far_down, weights, acc, acts):
    far = gathered((far_up, far_down))
    width = acts.shape[1]
    start = weights.shape[0] - far.shape[1]
    total = acc[...] + jnp.dot(far, weights[start:], preferred_element_type=jnp.float32)
    first, second, third = (total[:, k * width : (k + 1) * width] for k in range(3))
    gate = 1.0 / (1.0 + jnp.exp(-third))
    cubic = 0.7978845608 * (first + 0.044715 * (first * first * first))
    value = acts.astype(jnp.float32) + gate * (0.5 * first * (1.0 + jnp.tanh(cubic))) * second
    return value.astype(jnp.bfloat16)


def hand_on(parts, weights, acc, acts, injected, cut, after):
    def kernel(far_up, far_down, weights, acc, acts, injected, out):
        value = finished(far_up, far_down, weights, acc, acts[cut])
        last = lax.axis_index("section") == lax.axis_size("section") - 1
        out[...] = jnp.where(last, injected[cut], value)

    return run(
        kernel,
        pltpu.VMEM(parts[0].shape[1:], jnp.bfloat16),
        [*parts, weights, acc, acts, injected],
        after,
        megabytes=16,
    )


def conclude(parts, weights, acc, acts, before, after):
    def kernel(far_up, far_down, weights, acc, acts, *refs):
        out = refs[-1]
        done = 0
        for ref in refs[:-1]:
            out[done : done + ref.shape[0]] = ref[...]
            done += ref.shape[0]
        out[done:] = finished(far_up, far_down, weights, acc, acts[...])

    tokens, width = acts.shape
    tokens += sum(v.shape[0] for v in before)
    kind = pltpu.VMEM if not before else jax.ShapeDtypeStruct
    return run(
        kernel,
        kind((tokens, width), jnp.bfloat16),
        [*parts, weights, acc, acts, *before],
        after,
        megabytes=16,
    )


def second_phase(near):
    return shift(near, 1, False), shift(near, 3, False)


def third_phase(up, down, after):
    far_up, far_down = pick(up, down, after)
    return (shift(far_up, 1, False), shift(far_down, 3, False)), far_up


def body(in_flight, injected, weights):
    own = weights[0]
    other = lax.ppermute(own, "row", [(0, 1), (1, 0)])
    acts, injected = in_flight[0], injected[0]
    half = acts.shape[0] // 2
    low, high = slice(0, half), slice(half, 2 * half)
    whole = slice(0, half)

    blocks = [shift(acts, step, True) for step in (1, 3)]
    acts, injected = bring_in([acts, injected])
    blocks = [acts, *blocks, shift(acts, 2, True)]
    near_a = stack(blocks, low, [])
    moved_a = second_phase(near_a)
    arranged = arrange(own, other, [near_a])
    near_b = stack(blocks, high, [arranged])
    moved_b = second_phase(near_b)
    acc_a = nearest(near_a, arranged, [near_b])
    acc_b = nearest(near_b, arranged, [acc_a])
    far_a, sent = third_phase(*moved_a, [acc_b])
    acc_a = next_ones(*moved_a, arranged, acc_a, [sent])
    far_b, sent = third_phase(*moved_b, [acc_a])
    out_a = hand_on(far_a, arranged, acc_a, acts, injected, low, [sent])
    acc_b = next_ones(*moved_b, arranged, acc_b, [out_a])
    out_b = hand_on(far_b, arranged, acc_b, acts, injected, high, [])

    acts_a = same(relay(out_a), [out_b])
    acts_b = same(relay(out_b), [acts_a])
    blocks = [acts_a] + [shift(acts_a, step, True) for step in (1, 3, 2)]
    near_a = stack(blocks, whole, [acts_b])
    moved_a = second_phase(near_a)
    blocks = [acts_b] + [shift(acts_b, step, True) for step in (1, 3, 2)]
    near_b = stack(blocks, whole, [near_a])
    moved_b = second_phase(near_b)
    acc_a = nearest(near_a, arranged, [near_b])
    acc_b = nearest(near_b, arranged, [acc_a])
    far_a, sent = third_phase(*moved_a, [acc_b])
    acc_a = next_ones(*moved_a, arranged, acc_a, [sent])
    far_b, sent = third_phase(*moved_b, [acc_a])
    out_a = conclude(far_a, arranged, acc_a, acts_a, [], [sent])
    acc_b = next_ones(*moved_b, arranged, acc_b, [out_a])
    return conclude(far_b, arranged, acc_b, acts_b, [out_a], [])[None]


def solution(mesh):
    placed = (P("section", "row", "col"), P(None, "row", "col"), P("section", None, "row", "col"))
    return jax.shard_map(
        body, mesh=mesh, in_specs=placed, out_specs=P("section", "row", "col"), check_vma=False
    )
```

```python
import functools

import jax
import jax.numpy as jnp
from jax import lax
from jax.experimental import pallas as pl
from jax.experimental.pallas import tpu as pltpu
from jax.sharding import PartitionSpec as P

SIDE = 4
PLANE = ("row", "col")
NEAR = (0, -1, 1, 2)
HALF = 256
VMEM = pl.BlockSpec(memory_space=pltpu.VMEM)
ANY = pl.BlockSpec(memory_space=pl.ANY)


def ring_pairs(step, first):
    pairs = []
    for core in range(2):
        for col in range(SIDE * SIDE):
            y, x = divmod(col, SIDE)
            if (core == 0) == first:
                x = (x + step) % SIDE
            else:
                y = (y + step) % SIDE
            pairs.append((core * SIDE * SIDE + col, core * SIDE * SIDE + y * SIDE + x))
    return pairs


def shift(value, step, first):
    return lax.ppermute(value, PLANE, ring_pairs(step, first))


def relay(output):
    count = lax.axis_size("section")
    return lax.ppermute(output, "section", [(s, (s + 1) % count) for s in range(count)])


def block_ids():
    core, col = lax.axis_index("row"), lax.axis_index("col")
    y, x = col // SIDE, col % SIDE
    ids = []
    for second in NEAR:
        for first in NEAR:
            along_x = first + core * (second - first)
            along_y = second + core * (first - second)
            block = (y + along_y + SIDE) % SIDE * SIDE + (x + along_x + SIDE) % SIDE
            ids.append(((block // 8 + core) % 2, block % 8))
    return ids


def in_vmem(value):
    return pltpu.with_memory_space_constraint(value, pltpu.VMEM)


def in_hbm(value):
    return pltpu.with_memory_space_constraint(value, pltpu.HBM)


def run(kernel, out_shape, operands, after=(), specs=None, scratch=(), megabytes=4, place=VMEM):
    operands = list(operands)
    if specs is None:
        specs = [VMEM] * len(operands)
        operands = [in_vmem(v) for v in operands]
    count = len(operands)

    def body(*refs):
        kernel(*refs[:count], *refs[count + len(after) :])

    return pl.pallas_call(
        body,
        out_shape=out_shape,
        in_specs=specs + [VMEM] * len(after),
        out_specs=jax.tree.map(lambda _: place, out_shape),
        scratch_shapes=list(scratch),
        compiler_params=pltpu.CompilerParams(vmem_limit_bytes=megabytes * 1024 * 1024),
        cost_estimate=pl.CostEstimate(flops=1, bytes_accessed=1, transcendentals=0),
    )(*operands, *map(in_vmem, after))


def arrange(own, other, after):
    _, half, width = own.shape
    depth = half // 8

    def kernel(own, other, out, sems):
        ids = block_ids()

        def copy(source, block, k):
            rows = pl.ds(pl.multiple_of(ids[block][1] * depth, depth), depth)
            place = out.at[pl.ds(block * depth, depth), pl.ds(k * width, width)]
            return pltpu.make_async_copy(source.at[k, rows, :], place, sems.at[block, k])

        for block in range(SIDE * SIDE):

            @pl.when(ids[block][0] == 0)
            def _():
                for k in range(3):
                    copy(own, block, k).start()

            @pl.when(ids[block][0] != 0)
            def _():
                for k in range(3):
                    copy(other, block, k).start()

        for block in range(SIDE * SIDE):
            for k in range(3):
                copy(own, block, k).wait()

    return run(
        kernel,
        pltpu.VMEM((2 * half, 3 * width), jnp.bfloat16),
        [in_hbm(own), in_vmem(other)],
        after,
        specs=[ANY, VMEM],
        scratch=[pltpu.SemaphoreType.DMA((SIDE * SIDE, 3))],
    )


def bring_in(values):
    def kernel(*refs):
        sems = refs[-1]
        count = len(values)
        copies = [
            pltpu.make_async_copy(refs[i], refs[count + i], sems.at[i]) for i in range(count)
        ]
        for copy in copies:
            copy.start()
        for copy in copies:
            copy.wait()

    return run(
        kernel,
        tuple(pltpu.VMEM(v.shape, v.dtype) for v in values),
        [in_hbm(v) for v in values],
        specs=[ANY] * len(values),
        scratch=[pltpu.SemaphoreType.DMA((len(values),))],
    )


def stack(pieces, after):
    arrays, picks = operands_of(pieces)

    def kernel(*refs):
        for i, (n, what) in enumerate(picks):
            refs[-1][i] = refs[n][what]

    kind = pltpu.VMEM((len(pieces), HALF, arrays[0].shape[-1]), jnp.bfloat16)
    return run(kernel, kind, arrays, after)


def operands_of(pieces):
    arrays, picks = [], []
    for array, what in pieces:
        known = [n for n, other in enumerate(arrays) if other is array]
        if not known:
            arrays.append(array)
        picks.append((known[0] if known else len(arrays) - 1, what))
    return arrays, picks


def same(value, after):
    def kernel(value, out):
        out[...] = value[...]

    return run(kernel, pltpu.VMEM(value.shape, value.dtype), [value], after)


def products(refs, picks, weights, first):
    acts = jnp.concatenate([refs[n][what] for n, what in picks], axis=1)
    start = first * refs[0].shape[-1]
    return jnp.dot(acts, weights[start : start + acts.shape[1]], preferred_element_type=jnp.float32)


def partial(pieces, first, weights, acc, after):
    arrays, picks = operands_of(pieces)

    def kernel(*refs):
        value = products(refs, picks, refs[len(arrays)], first)
        refs[-1][...] = value if acc is None else refs[len(arrays) + 1][...] + value

    kind = pltpu.VMEM((HALF, 3 * arrays[0].shape[-1]), jnp.float32)
    operands = [*arrays, weights] + ([] if acc is None else [acc])
    return run(kernel, kind, operands, after, megabytes=16)


def finish(far, weights, acc, own, injected, before, after):
    arrays, picks = operands_of([(part, i) for part in far for i in range(2)])
    width = arrays[0].shape[-1]
    operands = [in_vmem(v) for v in (*arrays, weights, acc, own[0])]
    specs = [VMEM] * len(operands)
    scratch = []
    if injected is not None:
        operands.append(in_vmem(injected[0]))
        specs.append(VMEM)
    if before is not None:
        operands.append(in_vmem(before))
        specs.append(VMEM)
    if before is not None:
        scratch = [pltpu.VMEM((HALF, width), jnp.bfloat16), pltpu.SemaphoreType.DMA((2,))]

    def kernel(*refs):
        weights, acc, acts = refs[len(arrays) : len(arrays) + 3]
        out = refs[len(operands)]
        if scratch:
            kept, sems = refs[-2:]
        if before is not None:
            store = pltpu.make_async_copy(refs[len(operands) - 1], out.at[pl.ds(0, HALF)], sems.at[0])
            store.start()
        total = acc[...] + products(refs, picks, weights, 3 * SIDE)
        first, second, third = (total[:, k * width : (k + 1) * width] for k in range(3))
        gate = 1.0 / (1.0 + jnp.exp(-third))
        cubic = 0.7978845608 * (first + 0.044715 * (first * first * first))
        value = acts[own[1]].astype(jnp.float32)
        value += gate * (0.5 * first * (1.0 + jnp.tanh(cubic))) * second
        value = value.astype(jnp.bfloat16)
        if injected is not None:
            last = lax.axis_index("section") == lax.axis_size("section") - 1
            value = jnp.where(last, refs[len(operands) - 1][injected[1]], value)
        if before is None:
            out[...] = value
        else:
            kept[...] = value
            rest = pltpu.make_async_copy(kept, out.at[pl.ds(HALF, HALF)], sems.at[1])
            rest.start()
            store.wait()
            rest.wait()

    if before is None:
        kind, place = pltpu.VMEM((HALF, width), jnp.bfloat16), VMEM
    else:
        kind, place = jax.ShapeDtypeStruct((2 * HALF, width), jnp.bfloat16), ANY
    return run(kernel, kind, operands, after, specs=specs, scratch=scratch, megabytes=16, place=place)


def first_phase(acts):
    return [acts] + [shift(acts, step, True) for step in (1, 3, 2)]


def both_ways(value):
    return shift(value, 1, False), shift(value, 3, False)


def third_phase(up, down, after):
    arrays, picks = operands_of(up[:2] + down[2:])

    def kernel(*refs):
        for i, (n, what) in enumerate(picks):
            refs[len(arrays) + i // 2][i % 2] = refs[n][what]

    kind = pltpu.VMEM((2, HALF, arrays[0].shape[-1]), jnp.bfloat16)
    one, two = run(kernel, (kind, kind), arrays, after)
    return (shift(one, 1, False), shift(two, 3, False)), one


def body(in_flight, injected, weights):
    own = weights[0]
    other = lax.ppermute(own, "row", [(0, 1), (1, 0)])
    low, high = slice(0, HALF), slice(HALF, 2 * HALF)
    every = slice(0, HALF)

    near = [shift(in_flight[0], step, True) for step in (1, 3)]
    acts, injected = bring_in([in_flight[0], injected[0]])
    near = [*near, shift(acts, 2, True)]
    near_a = stack([(block, low) for block in [acts, *near]], [])
    up, down = both_ways(near_a)
    up_a = [(up, i) for i in range(SIDE)]
    down_a = [(down, i) for i in range(SIDE)]
    near_a = [(near_a, i) for i in range(SIDE)]
    arranged = arrange(own, other, [near_a[0][0]])
    near_b = stack([(block, high) for block in [acts, *near]], [arranged])
    up, down = both_ways(near_b)
    up_b = [(up, i) for i in range(SIDE)]
    down_b = [(down, i) for i in range(SIDE)]
    near_b = [(near_b, i) for i in range(SIDE)]
    acc_a = partial(near_a, 0, arranged, None, [near_b[0][0]])
    acc_b = partial(near_b, 0, arranged, None, [acc_a])
    far_a, sent = third_phase(up_a, down_a, [acc_b])
    acc_a = partial(up_a + down_a, SIDE, arranged, acc_a, [sent])
    far_b, sent = third_phase(up_b, down_b, [acc_a])
    out_a = finish(far_a, arranged, acc_a, near_a[0], (injected, low), None, [sent])
    acc_b = partial(up_b + down_b, SIDE, arranged, acc_b, [out_a])
    out_b = finish(far_b, arranged, acc_b, near_b[0], (injected, high), None, [])

    acts_a = relay(out_a)
    acts_b = relay(out_b)
    near_a = stack([(block, every) for block in first_phase(acts_a)], [acts_b])
    up, down = both_ways(near_a)
    up_a = [(up, i) for i in range(SIDE)]
    down_a = [(down, i) for i in range(SIDE)]
    near_a = [(near_a, i) for i in range(SIDE)]
    near_b = stack([(block, every) for block in first_phase(acts_b)], [near_a[0][0]])
    up, down = both_ways(near_b)
    up_b = [(up, i) for i in range(SIDE)]
    down_b = [(down, i) for i in range(SIDE)]
    near_b = [(near_b, i) for i in range(SIDE)]
    acc_a = partial(near_a, 0, arranged, None, [near_b[0][0]])
    acc_b = partial(near_b, 0, arranged, None, [acc_a])
    far_a, sent = third_phase(up_a, down_a, [acc_b])
    acc_a = partial(up_a + down_a, SIDE, arranged, acc_a, [sent])
    far_b, sent = third_phase(up_b, down_b, [acc_a])
    out_a = finish(far_a, arranged, acc_a, near_a[0], None, None, [sent])
    acc_b = partial(up_b + down_b, SIDE, arranged, acc_b, [out_a])
    return finish(far_b, arranged, acc_b, near_b[0], None, out_a, [])[None]


def solution(mesh):
    placed = (P("section", "row", "col"), P(None, "row", "col"), P("section", None, "row", "col"))
    return jax.shard_map(
        body, mesh=mesh, in_specs=placed, out_specs=P("section", "row", "col"), check_vma=False
    )
```
